32 devices in a mesh: ctx: 16 (over z, y, x), grp: 2 (over core).
Axes of the slice: x: 2, y: 2, z: 4, core: 2. Of those that a mesh axis runs over, the one named last changes fastest.
Arguments:
- tokens: bfloat16 [8192, 4096], P('ctx'), may hold values from -6 to 6
- w_z: bfloat16 [4096, 8192], P('ctx', 'grp'), may hold values from -0.09375 to 0.09375
- w_x: bfloat16 [4096, 8192], P('ctx', 'grp'), may hold values from -0.09375 to 0.09375
- w_bc: bfloat16 [4096, 8, 256], P('ctx', 'grp'), may hold values from -0.09375 to 0.09375
- w_dt: bfloat16 [4096, 128], P('ctx', 'grp'), may hold values from -0.09375 to 0.09375
- conv_x: float32 [4, 8192], P(None, 'grp'), may hold values from -3 to 3
- conv_bc: float32 [4, 8, 256], P(None, 'grp'), may hold values from -3 to 3
- bias_x: float32 [8192], P('grp'), may hold values from -3 to 3
- bias_bc: float32 [8, 256], P('grp'), may hold values from -3 to 3
- dt_bias: float32 [128], P('grp'), may hold values from -5.3 to -3
- a_log: float32 [128], P('grp'), as said below
- d_skip: float32 [128], P('grp'), may hold values from 0.5 to 1.5
- norm_gain: float32 [8192], P('grp'), may hold values from 0.5 to 1.5
Outputs:
- layer_out: bfloat16 [8192, 8192], P('ctx', 'grp')
The draws below stay inside these ranges and needn't reach their ends.
Inputs may be any that keep to these rules, and one draw needn't show every extreme that they name: `a_log`: each head's log decay rate; some heads forget within tens of tokens, others keep much of their state over all 8192 tokens.
All inputs are finite; a program needn't handle non-finite values.
Results may differ from the reference program's by a relative error of at most 0.013.
Values may be sent and summed in bfloat16 or wider, within the bound.
A program may use at most 192 MiB of HBM per device.

```python
import math
import jax
import jax.numpy as jnp
from jax import lax

D = 4096
HEADS = 128
HEAD_DIM = 64
STATE = 128
GROUPS = 8
CONV = 4
SPAN = 256
TOKENS = 8192


def draw_a_log(key, part):
    key_pick, key_fast, key_slow = jax.random.split(jax.random.fold_in(key, 11), 3)
    fast_share = 0.5
    picked = jax.random.uniform(key_pick, (HEADS,), jnp.float32) < fast_share
    fast_log = jax.random.uniform(key_fast, (HEADS,), jnp.float32, 0.0, 3.0)
    slow_log = jax.random.uniform(key_slow, (HEADS,), jnp.float32, math.log(0.3), math.log(2.0)) - math.log(0.02 * TOKENS)
    return jnp.where(picked, fast_log, slow_log).astype(jnp.float32)


def steps_of(key, extent, cuts, low, top_value):
    factor_of, own = 1.0, jax.random.fold_in(key, 6)
    for position, shards_of in cuts:
        heights = jnp.exp(jax.random.uniform(jax.random.fold_in(own, position), (shards_of,), jnp.float32, low / len(cuts), top_value / len(cuts)))
        factor_of = factor_of * jnp.repeat(heights, extent[position] // shards_of).reshape([-1 if axis == position else 1 for axis in range(len(extent))])
    return factor_of


def bell_draw(own_key, extent, width, bound, cuts=(), dtype=jnp.bfloat16):
    values = width * jax.random.normal(own_key, extent, jnp.float32)
    if cuts:
        values = values * steps_of(own_key, extent, cuts, -0.22, 0.18)
    return jnp.clip(values, -bound, bound).astype(dtype)


def setup_inputs(seed: int = 0) -> dict:
    keys = jax.random.split(jax.random.key(seed), 14)
    return {
        "tokens": bell_draw(keys[0], (TOKENS, D), 1.0, 6.0, ((0, 16),)),
        "w_z": bell_draw(keys[1], (D, HEADS * HEAD_DIM), D ** -0.5, 0.09375, ((0, 16), (1, 2))),
        "w_x": bell_draw(keys[2], (D, HEADS * HEAD_DIM), D ** -0.5, 0.09375, ((0, 16), (1, 2))),
        "w_bc": bell_draw(keys[3], (D, GROUPS, 2 * STATE), D ** -0.5, 0.09375, ((0, 16), (1, 2))),
        "w_dt": bell_draw(keys[4], (D, HEADS), D ** -0.5, 0.09375, ((0, 16), (1, 2))),
        "conv_x": bell_draw(keys[5], (CONV, HEADS * HEAD_DIM), CONV ** -0.5, 3.0, ((1, 2),), jnp.float32),
        "conv_bc": bell_draw(keys[6], (CONV, GROUPS, 2 * STATE), CONV ** -0.5, 3.0, ((1, 2),), jnp.float32),
        "bias_x": bell_draw(keys[7], (HEADS * HEAD_DIM,), 0.5, 3.0, ((0, 2),), jnp.float32),
        "bias_bc": bell_draw(keys[8], (GROUPS, 2 * STATE), 0.5, 3.0, ((0, 2),), jnp.float32),
        "dt_bias": jnp.clip(-5.3 + 2.3000002 * jax.random.uniform(keys[9], (HEADS,), jnp.float32) ** steps_of(keys[9], (HEADS,), ((0, 2),), -0.2, 0.2), -5.3, -3.0),
        "a_log": draw_a_log(jax.random.fold_in(keys[13], 71), 0),
        "d_skip": jnp.clip(0.5 + 1.0 * jax.random.uniform(keys[11], (HEADS,), jnp.float32) ** steps_of(keys[11], (HEADS,), ((0, 2),), -0.2, 0.2), 0.5, 1.5),
        "norm_gain": jnp.clip(1.0 + 0.1 * jax.random.normal(keys[12], (HEADS * HEAD_DIM,), jnp.float32), 0.5, 1.5),
    }


def causal_taps(extended, taps, offset_bias):
    running = jnp.zeros((SPAN, taps.shape[1]), jnp.float32) + offset_bias[None, :]
    for tap in range(CONV):
        running = running + taps[tap][None, :] * extended[tap:tap + SPAN].astype(jnp.float32)
    return jax.nn.silu(running).astype(jnp.bfloat16)

def reference(tokens, w_z, w_x, w_bc, w_dt, conv_x, conv_bc, bias_x, bias_bc, dt_bias, a_log, d_skip, norm_gain):
    per_group = HEADS // GROUPS
    bc_width = GROUPS * 2 * STATE
    inner_width = HEADS * HEAD_DIM
    w_mix = w_bc.reshape(D, bc_width)
    conv_mix = conv_bc.reshape(CONV, bc_width)
    bias_mix = bias_bc.reshape(bc_width)
    decay_rate = jnp.exp(a_log)
    causal_mask = jnp.arange(SPAN)[:, None] >= jnp.arange(SPAN)[None, :]

    def advance(carry, block_tokens):
        state, prev_inner, prev_mix = carry
        gate_rows = jnp.dot(block_tokens, w_z, preferred_element_type=jnp.float32).astype(jnp.bfloat16)
        inner = jnp.dot(block_tokens, w_x, preferred_element_type=jnp.float32).astype(jnp.bfloat16)
        mixed = jnp.dot(block_tokens, w_mix, preferred_element_type=jnp.float32).astype(jnp.bfloat16)
        step_raw = jnp.dot(block_tokens, w_dt, preferred_element_type=jnp.float32)
        inner_c = causal_taps(jnp.concatenate([prev_inner, inner], axis=0), conv_x, bias_x)
        mix_c = causal_taps(jnp.concatenate([prev_mix, mixed], axis=0), conv_mix, bias_mix)
        mix_c = mix_c.reshape(SPAN, GROUPS, 2 * STATE)
        b_in = mix_c[:, :, :STATE].astype(jnp.float32)
        c_in = mix_c[:, :, STATE:].astype(jnp.float32)
        step_size = jax.nn.softplus(step_raw + dt_bias[None, :])
        cumul = jnp.cumsum(-decay_rate[None, :] * step_size, axis=0)
        scores = jnp.einsum('ign,jgn->gij', c_in, b_in)
        scores_h = jnp.repeat(scores, per_group, axis=0)
        cumul_t = cumul.T
        log_gap = cumul_t[:, :, None] - cumul_t[:, None, :]
        decay_mat = jnp.where(causal_mask[None], jnp.exp(jnp.minimum(log_gap, 0.0)), 0.0)
        weight = (scores_h * decay_mat * step_size.T[:, None, :]).astype(jnp.bfloat16)
        inner_h = inner_c.reshape(SPAN, HEADS, HEAD_DIM).astype(jnp.float32)
        intra = jnp.einsum('hij,jhp->ihp', weight.astype(jnp.float32), inner_h)
        c_heads = jnp.repeat(c_in, per_group, axis=1)
        inter = jnp.einsum('ihn,hnp->ihp', c_heads, state, precision=lax.Precision.HIGHEST) * jnp.exp(cumul)[:, :, None]
        scan_out = intra + inter + d_skip[None, :, None] * inner_h
        block_log = cumul[-1]
        b_heads = jnp.repeat(b_in, per_group, axis=1)
        weighted_b = ((jnp.exp(block_log[None, :] - cumul) * step_size)[:, :, None] * b_heads).astype(jnp.bfloat16)
        local_state = jnp.einsum('jhn,jhp->hnp', weighted_b.astype(jnp.float32), inner_h)
        new_state = jnp.exp(block_log)[:, None, None] * state + local_state
        gated = scan_out.reshape(SPAN, inner_width) * jax.nn.silu(gate_rows.astype(jnp.float32))
        grouped = gated.reshape(SPAN, GROUPS, per_group * HEAD_DIM)
        scale = lax.rsqrt(lax.optimization_barrier(jnp.mean(grouped * grouped, axis=-1, keepdims=True)) + 1e-05)
        result = ((grouped * scale).reshape(SPAN, inner_width) * norm_gain[None, :]).astype(jnp.bfloat16)
        return ((new_state, inner[SPAN - (CONV - 1):], mixed[SPAN - (CONV - 1):]), result)
    init = (jnp.zeros((HEADS, STATE, HEAD_DIM), jnp.float32), jnp.zeros((CONV - 1, inner_width), jnp.bfloat16), jnp.zeros((CONV - 1, bc_width), jnp.bfloat16))
    blocks = tokens.reshape(TOKENS // SPAN, SPAN, D)
    final_carry, results = lax.scan(advance, init, blocks)
    return results.reshape(TOKENS, inner_width)
```

```python
import jax
import jax.numpy as jnp
from jax import lax
from jax.sharding import PartitionSpec as P

SPAN = 256
F32 = jnp.float32
BF16 = jnp.bfloat16


def exchange_columns(value, groups, count):
    if count == 1:
        return value
    rows = value.shape[0]
    parts = value.reshape(rows, count, -1)
    got = lax.all_to_all(
        parts.swapaxes(0, 1), "ctx", 0, 0, axis_index_groups=groups, tiled=True
    )
    return got.reshape(count * rows, -1)


def on_device(
    tokens,
    w_z,
    w_x,
    w_bc,
    w_dt,
    conv_x,
    conv_bc,
    bias_x,
    bias_bc,
    dt_bias,
    a_log,
    d_skip,
    norm_gain,
):
    own_rows = tokens.shape[0]
    kernel = conv_x.shape[0]
    group_count = w_bc.shape[1]
    bc_width = w_bc.shape[2]
    state_size = bc_width // 2
    heads = w_dt.shape[1] // group_count
    width = w_x.shape[1] // group_count
    head_dim = width // heads
    devices = lax.axis_size("ctx")
    plane = group_count
    depth = devices // plane
    mine = lax.axis_index("ctx")
    column, level = mine % plane, mine // plane
    in_plane = [[z * plane + i for i in range(plane)] for z in range(depth)]
    along = [[z * plane + i for z in range(depth)] for i in range(plane)]

    def take(value):
        size = value.shape[-1] // plane
        return lax.dynamic_slice_in_dim(value, column * size, size, axis=value.ndim - 1)

    k_rows = w_x.shape[0]
    main = jnp.concatenate(
        [
            w_x.reshape(k_rows, plane, width),
            w_bc,
            w_dt.reshape(k_rows, plane, heads),
        ],
        axis=2,
    ).reshape(k_rows, -1)
    main = exchange_columns(main, in_plane, plane)
    main = lax.all_gather(main, "ctx", axis=0, tiled=True, axis_index_groups=along)
    if plane > 1:
        toks = lax.all_gather(tokens, "ctx", axis=0, tiled=True, axis_index_groups=in_plane)
    else:
        toks = tokens
    w_gate = exchange_columns(w_z, in_plane, plane)
    w_gate = lax.all_gather(w_gate, "ctx", axis=0, tiled=True, axis_index_groups=along)
    rows = toks.shape[0]
    blocks = rows // SPAN

    projected = jnp.dot(toks, main, preferred_element_type=F32)
    step_sum = projected[:, width + bc_width :]
    mixed = projected[:, : width + bc_width].astype(BF16)
    edge = lax.ppermute(
        mixed[rows - (kernel - 1) :],
        "ctx",
        [(i, i + plane) for i in range(devices - plane)],
    )
    extended = jnp.concatenate([edge, mixed], axis=0)
    taps = jnp.concatenate([take(conv_x), take(conv_bc.reshape(kernel, -1))], axis=1)
    offset = jnp.concatenate([take(bias_x), take(bias_bc.reshape(-1))])
    running = jnp.zeros((rows, width + bc_width), F32) + offset[None, :]
    for tap in range(kernel):
        running = running + taps[tap][None, :] * extended[tap : tap + rows].astype(F32)
    conv = jax.nn.silu(running).astype(BF16)
    inner = conv[:, :width].reshape(blocks, SPAN, heads, head_dim)
    b_in = conv[:, width : width + state_size].reshape(blocks, SPAN, state_size)
    c_in = conv[:, width + state_size :].reshape(blocks, SPAN, state_size)

    step = jax.nn.softplus(step_sum + take(dt_bias)[None, :])
    log_rate = -jnp.exp(take(a_log))[None, :] * step
    cumul = jnp.cumsum(log_rate.reshape(blocks, SPAN, heads), axis=1)
    step = step.reshape(blocks, SPAN, heads)
    scores = jnp.einsum("cin,cjn->cij", c_in, b_in, preferred_element_type=F32)
    cumul_t = jnp.swapaxes(cumul, 1, 2)
    step_t = jnp.swapaxes(step, 1, 2)
    gap = cumul_t[:, :, :, None] - cumul_t[:, :, None, :]
    causal = jnp.arange(SPAN)[:, None] >= jnp.arange(SPAN)[None, :]
    decay = jnp.where(causal[None, None], jnp.exp(jnp.minimum(gap, 0.0)), 0.0)
    weight = (scores[:, None] * decay * step_t[:, :, None, :]).astype(BF16)
    intra = jnp.einsum("chij,cjhp->cihp", weight, inner, preferred_element_type=F32)
    block_log = cumul[:, -1, :]
    weighted_b = (
        (jnp.exp(block_log[:, None, :] - cumul) * step)[..., None]
        * b_in[:, :, None, :].astype(F32)
    ).astype(BF16)
    local = jnp.einsum("cjhn,cjhp->chnp", weighted_b, inner, preferred_element_type=F32)
    state = jnp.zeros((heads, state_size, head_dim), F32)
    before = jnp.zeros((heads,), F32)
    starts, befores = [], []
    for block in range(blocks):
        starts.append(state)
        befores.append(before)
        state = jnp.exp(block_log[block])[:, None, None] * state + local[block]
        before = before + block_log[block]
    starts = jnp.stack(starts).astype(BF16)
    inter = jnp.einsum("cin,chnp->cihp", c_in, starts, preferred_element_type=F32)
    scan = (
        intra
        + inter * jnp.exp(cumul)[..., None]
        + take(d_skip)[None, None, :, None] * inner.astype(F32)
    ).reshape(rows, width)
    reach = jnp.exp(cumul + jnp.stack(befores)[:, None, :]).reshape(rows, heads)

    high = lax.reduce_precision(before, 8, 7)
    low = before - high
    logs = jnp.stack([high, low]).astype(BF16)
    packed = jnp.concatenate(
        [
            state.transpose(1, 0, 2).reshape(state_size, width).astype(BF16),
            jnp.repeat(logs, head_dim, axis=1),
        ]
    )
    everyone = lax.all_gather(packed, "ctx", axis_index_groups=along)
    all_logs = (
        everyone[:, state_size].astype(F32) + everyone[:, state_size + 1].astype(F32)
    )
    order = jnp.arange(depth)
    between = (order[None, :] > order[:, None]) & (order[None, :] < level)
    factor = jnp.exp(jnp.sum(jnp.where(between[:, :, None], all_logs[None], 0.0), axis=1))
    factor = jnp.where((order < level)[:, None], factor, 0.0)
    carried = jnp.sum(everyone[:, :state_size].astype(F32) * factor[:, None, :], axis=0)
    far = jnp.dot(
        c_in.reshape(rows, state_size), carried.astype(BF16), preferred_element_type=F32
    )
    scan = (
        scan.reshape(rows, heads, head_dim)
        + far.reshape(rows, heads, head_dim) * reach[:, :, None]
    ).reshape(rows, width)

    gate = jnp.dot(toks, w_gate, preferred_element_type=F32).astype(BF16).astype(F32)
    gated = scan * jax.nn.silu(gate)
    scale = lax.rsqrt(jnp.mean(gated * gated, axis=-1, keepdims=True) + 1e-05)
    result = (gated * scale * take(norm_gain)[None, :]).astype(BF16)
    if plane == 1:
        return result
    back = lax.all_to_all(
        result.reshape(plane, own_rows, width), "ctx", 0, 0, axis_index_groups=in_plane, tiled=True
    )
    return back.swapaxes(0, 1).reshape(own_rows, plane * width)


def solution(mesh):
    placed = (
        P("ctx", None),
        P("ctx", "grp"),
        P("ctx", "grp"),
        P("ctx", "grp", None),
        P("ctx", "grp"),
        P(None, "grp"),
        P(None, "grp", None),
        P("grp"),
        P("grp", None),
        P("grp"),
        P("grp"),
        P("grp"),
        P("grp"),
    )
    return jax.shard_map(
        on_device, mesh=mesh, in_specs=placed, out_specs=P("ctx", "grp"), check_vma=False
    )
```

```python
import jax
import jax.numpy as jnp
from jax import lax
from jax.sharding import PartitionSpec as P

SPAN = 256
F32 = jnp.float32
BF16 = jnp.bfloat16


def exchange_columns(value, groups, count):
    if count == 1:
        return value
    rows = value.shape[0]
    parts = value.reshape(rows, count, -1)
    got = lax.all_to_all(
        parts.swapaxes(0, 1), "ctx", 0, 0, axis_index_groups=groups, tiled=True
    )
    return got.reshape(count * rows, -1)


def swapped(value, step, plane):
    pairs = [(i, i - i % plane + (i % plane ^ step)) for i in range(lax.axis_size("ctx"))]
    return lax.ppermute(value, "ctx", pairs)


def earlier_parts(value, along, plane, depth):
    if depth <= 4:
        for back in range(1, depth):
            pairs = [(i, i + back * plane) for i in range((depth - back) * plane)]
            yield lax.ppermute(value, "ctx", pairs)
    else:
        everyone = lax.all_gather(value, "ctx", axis_index_groups=along)
        level = lax.axis_index("ctx") // plane
        for back in range(1, depth):
            part = lax.dynamic_index_in_dim(
                everyone, jnp.maximum(level - back, 0), keepdims=False
            )
            yield jnp.where(back <= level, part, 0)


def on_device(
    tokens,
    w_z,
    w_x,
    w_bc,
    w_dt,
    conv_x,
    conv_bc,
    bias_x,
    bias_bc,
    dt_bias,
    a_log,
    d_skip,
    norm_gain,
):
    own_rows = tokens.shape[0]
    kernel = conv_x.shape[0]
    group_count = w_bc.shape[1]
    bc_width = w_bc.shape[2]
    state_size = bc_width // 2
    heads = w_dt.shape[1] // group_count
    width = w_x.shape[1] // group_count
    head_dim = width // heads
    devices = lax.axis_size("ctx")
    plane = group_count
    depth = devices // plane
    mine = lax.axis_index("ctx")
    column = mine % plane
    in_plane = [[z * plane + i for i in range(plane)] for z in range(depth)]
    along = [[z * plane + i for z in range(depth)] for i in range(plane)]

    def take(value):
        size = value.shape[-1] // plane
        return lax.dynamic_slice_in_dim(value, column * size, size, axis=value.ndim - 1)

    k_rows = w_x.shape[0]
    main = jnp.concatenate(
        [
            w_x.reshape(k_rows, plane, width),
            w_bc,
            w_dt.reshape(k_rows, plane, heads),
        ],
        axis=2,
    ).reshape(k_rows, -1)
    main = exchange_columns(main, in_plane, plane)
    main, tokens, w_z = lax.optimization_barrier((main, tokens, w_z))
    main = lax.all_gather(main, "ctx", axis=0, tiled=True, axis_index_groups=along)
    pieces = [tokens] + [swapped(tokens, step, plane) for step in range(1, plane)]
    w_gate = exchange_columns(w_z, in_plane, plane)
    w_gate = lax.all_gather(w_gate, "ctx", axis=0, tiled=True, axis_index_groups=along)
    rows = own_rows * plane
    blocks = rows // SPAN

    mixed = jnp.zeros((rows, width + bc_width), BF16)
    step_sum = jnp.zeros((rows, heads), F32)
    for step, piece in enumerate(pieces):
        projected = jnp.dot(piece, main, preferred_element_type=F32)
        at = ((column ^ step) * own_rows, 0)
        mixed = lax.dynamic_update_slice(
            mixed, projected[:, : width + bc_width].astype(BF16), at
        )
        step_sum = lax.dynamic_update_slice(step_sum, projected[:, width + bc_width :], at)
    edge = lax.ppermute(
        mixed[rows - (kernel - 1) :],
        "ctx",
        [(i, i + plane) for i in range(devices - plane)],
    )
    extended = jnp.concatenate([edge, mixed], axis=0)
    taps = jnp.concatenate([take(conv_x), take(conv_bc.reshape(kernel, -1))], axis=1)
    offset = jnp.concatenate([take(bias_x), take(bias_bc.reshape(-1))])
    running = jnp.zeros((rows, width + bc_width), F32) + offset[None, :]
    for tap in range(kernel):
        running = running + taps[tap][None, :] * extended[tap : tap + rows].astype(F32)
    conv = jax.nn.silu(running).astype(BF16)
    inner = conv[:, :width].reshape(blocks, SPAN, heads, head_dim)
    b_in = conv[:, width : width + state_size].reshape(blocks, SPAN, state_size)
    c_in = conv[:, width + state_size :].reshape(blocks, SPAN, state_size)

    step = jax.nn.softplus(step_sum + take(dt_bias)[None, :])
    log_rate = -jnp.exp(take(a_log))[None, :] * step
    cumul = jnp.cumsum(log_rate.reshape(blocks, SPAN, heads), axis=1)
    step = step.reshape(blocks, SPAN, heads)
    scores = jnp.einsum("cin,cjn->cij", c_in, b_in, preferred_element_type=F32)
    cumul_t = jnp.swapaxes(cumul, 1, 2)
    step_t = jnp.swapaxes(step, 1, 2)
    gap = cumul_t[:, :, :, None] - cumul_t[:, :, None, :]
    causal = jnp.arange(SPAN)[:, None] >= jnp.arange(SPAN)[None, :]
    decay = jnp.where(causal[None, None], jnp.exp(jnp.minimum(gap, 0.0)), 0.0)
    weight = (scores[:, None] * decay * step_t[:, :, None, :]).astype(BF16)
    intra = jnp.einsum("chij,cjhp->cihp", weight, inner, preferred_element_type=F32)
    block_log = cumul[:, -1, :]
    weighted_b = (
        (jnp.exp(block_log[:, None, :] - cumul) * step)[..., None]
        * b_in[:, :, None, :].astype(F32)
    ).astype(BF16)
    local = jnp.einsum("cjhn,cjhp->chnp", weighted_b, inner, preferred_element_type=F32)
    state = jnp.zeros((heads, state_size, head_dim), F32)
    before = jnp.zeros((heads,), F32)
    starts, befores = [], []
    for block in range(blocks):
        starts.append(state)
        befores.append(before)
        state = jnp.exp(block_log[block])[:, None, None] * state + local[block]
        before = before + block_log[block]
    starts = jnp.stack(starts).astype(BF16)
    inter = jnp.einsum("cin,chnp->cihp", c_in, starts, preferred_element_type=F32)
    scan = (
        intra
        + inter * jnp.exp(cumul)[..., None]
        + take(d_skip)[None, None, :, None] * inner.astype(F32)
    ).reshape(rows, width)
    reach = jnp.exp(cumul + jnp.stack(befores)[:, None, :]).reshape(rows, heads)

    high = lax.reduce_precision(before, 8, 7)
    low = before - high
    logs = jnp.stack([high, low]).astype(BF16)
    packed = jnp.concatenate(
        [
            state.transpose(1, 0, 2).reshape(state_size, width).astype(BF16),
            jnp.repeat(logs, head_dim, axis=1),
        ]
    )
    carried = jnp.zeros((state_size, width), F32)
    skipped = jnp.zeros((width,), F32)
    for part in earlier_parts(packed, along, plane, depth):
        part = part.astype(F32)
        carried = carried + jnp.exp(skipped)[None, :] * part[:state_size]
        skipped = skipped + part[state_size] + part[state_size + 1]
    far = jnp.dot(
        c_in.reshape(rows, state_size), carried.astype(BF16), preferred_element_type=F32
    )
    scan = (
        scan.reshape(rows, heads, head_dim)
        + far.reshape(rows, heads, head_dim) * reach[:, :, None]
    ).reshape(rows, width)

    scan, w_gate = lax.optimization_barrier((scan, w_gate))
    gain = take(norm_gain)[None, :]
    out = jnp.zeros((own_rows, plane * width), BF16)
    for step in reversed(range(plane)):
        gate = jnp.dot(pieces[step], w_gate, preferred_element_type=F32).astype(BF16)
        part = lax.dynamic_slice_in_dim(scan, (column ^ step) * own_rows, own_rows)
        gated = part * jax.nn.silu(gate.astype(F32))
        scale = lax.rsqrt(jnp.mean(gated * gated, axis=-1, keepdims=True) + 1e-05)
        result = (gated * scale * gain).astype(BF16)
        if step:
            result = swapped(result, step, plane)
        out = lax.dynamic_update_slice(out, result, (0, (column ^ step) * width))
    return out


def solution(mesh):
    placed = (
        P("ctx", None),
        P("ctx", "grp"),
        P("ctx", "grp"),
        P("ctx", "grp", None),
        P("ctx", "grp"),
        P(None, "grp"),
        P(None, "grp", None),
        P("grp"),
        P("grp", None),
        P("grp"),
        P("grp"),
        P("grp"),
        P("grp"),
    )
    return jax.shard_map(
        on_device, mesh=mesh, in_specs=placed, out_specs=P("ctx", "grp"), check_vma=False
    )
```

```python
import functools

import jax
import jax.numpy as jnp
from jax import lax
from jax.experimental import pallas as pl
from jax.experimental.pallas import tpu as pltpu
from jax.sharding import PartitionSpec as P

SPAN = 256
F32 = jnp.float32
BF16 = jnp.bfloat16


def exchange_columns(value, groups, count):
    if count == 1:
        return value
    rows = value.shape[0]
    parts = value.reshape(rows, count, -1)
    got = lax.all_to_all(
        parts.swapaxes(0, 1), "ctx", 0, 0, axis_index_groups=groups, tiled=True
    )
    return got.reshape(count * rows, -1)


def swapped(value, step, plane):
    pairs = [(i, i - i % plane + (i % plane ^ step)) for i in range(lax.axis_size("ctx"))]
    return lax.ppermute(value, "ctx", pairs)


def earlier_parts(value, along, plane, depth):
    if depth <= 4:
        for back in range(1, depth):
            pairs = [(i, i + back * plane) for i in range((depth - back) * plane)]
            yield lax.ppermute(value, "ctx", pairs)
    else:
        everyone = lax.all_gather(value, "ctx", axis_index_groups=along)
        level = lax.axis_index("ctx") // plane
        for back in range(1, depth):
            part = lax.dynamic_index_in_dim(
                everyone, jnp.maximum(level - back, 0), keepdims=False
            )
            yield jnp.where(back <= level, part, 0)


def scan_body(
    width, state_size, conv, cumul, cumul_t, step_t, ending, decay, skip, out, state
):
    @pl.when(pl.program_id(0) == 0)
    def _():
        state[...] = jnp.zeros_like(state)

    b_in = conv[:, width : width + state_size]
    c_in = conv[:, width + state_size :]
    scores = lax.dot_general(
        c_in, b_in, (((1,), (1,)), ((), ())), preferred_element_type=F32
    )
    row = lax.broadcasted_iota(jnp.int32, (SPAN, SPAN), 0)
    col = lax.broadcasted_iota(jnp.int32, (SPAN, SPAN), 1)
    scores = jnp.where(row >= col, scores, 0.0)
    first = lax.broadcasted_iota(jnp.int32, (SPAN, 128), 1) < 64
    for pair in range(width // 128):
        lanes = slice(pair * 128, pair * 128 + 128)
        x_in = conv[:, lanes]
        x_wide = x_in.astype(F32)
        sums = []
        for head in (2 * pair, 2 * pair + 1):
            gap = cumul[:, head : head + 1] - cumul_t[0, head : head + 1, :]
            weight = scores * jnp.exp(jnp.minimum(gap, 0.0)) * step_t[0, head : head + 1, :]
            sums.append(jnp.dot(weight.astype(BF16), x_in, preferred_element_type=F32))

        def both(ref):
            return jnp.where(
                first, ref[:, 2 * pair : 2 * pair + 1], ref[:, 2 * pair + 1 : 2 * pair + 2]
            )

        old = state[:, lanes]
        inter = jnp.dot(c_in, old.astype(BF16), preferred_element_type=F32)
        out[:, lanes] = (
            jnp.where(first, sums[0], sums[1])
            + inter * jnp.exp(both(cumul))
            + skip[:, lanes] * x_wide
        )
        scaled = (x_wide * both(ending)).astype(BF16)
        new = lax.dot_general(
            b_in, scaled, (((0,), (0,)), ((), ())), preferred_element_type=F32
        )
        state[:, lanes] = decay[0, :, lanes] * old + new


def local_scan(
    conv, cumul, cumul_t, step_t, ending, decay, skip, width, state_size, heads
):
    rows = conv.shape[0]
    return pl.pallas_call(
        functools.partial(scan_body, width, state_size),
        grid=(rows // SPAN,),
        in_specs=[
            pl.BlockSpec((SPAN, conv.shape[1]), lambda i: (i, 0)),
            pl.BlockSpec((SPAN, heads), lambda i: (i, 0)),
            pl.BlockSpec((1, heads, SPAN), lambda i: (i, 0, 0)),
            pl.BlockSpec((1, heads, SPAN), lambda i: (i, 0, 0)),
            pl.BlockSpec((SPAN, heads), lambda i: (i, 0)),
            pl.BlockSpec((1, 1, width), lambda i: (i, 0, 0)),
            pl.BlockSpec((1, width), lambda i: (0, 0)),
        ],
        out_specs=[
            pl.BlockSpec((SPAN, width), lambda i: (i, 0)),
            pl.BlockSpec((state_size, width), lambda i: (0, 0)),
        ],
        out_shape=[
            jax.ShapeDtypeStruct((rows, width), F32),
            jax.ShapeDtypeStruct((state_size, width), F32),
        ],
        compiler_params=pltpu.CompilerParams(vmem_limit_bytes=32 * 1024 * 1024),
        cost_estimate=pl.CostEstimate(
            flops=2 * rows * width * (SPAN + 2 * state_size),
            bytes_accessed=rows * width * 8,
            transcendentals=rows * SPAN * heads,
        ),
        name="local_scan",
    )(conv, cumul, cumul_t, step_t, ending, decay, skip)


def on_device(
    tokens,
    w_z,
    w_x,
    w_bc,
    w_dt,
    conv_x,
    conv_bc,
    bias_x,
    bias_bc,
    dt_bias,
    a_log,
    d_skip,
    norm_gain,
):
    own_rows = tokens.shape[0]
    kernel = conv_x.shape[0]
    group_count = w_bc.shape[1]
    bc_width = w_bc.shape[2]
    state_size = bc_width // 2
    heads = w_dt.shape[1] // group_count
    width = w_x.shape[1] // group_count
    head_dim = width // heads
    devices = lax.axis_size("ctx")
    plane = group_count
    depth = devices // plane
    mine = lax.axis_index("ctx")
    column = mine % plane
    in_plane = [[z * plane + i for i in range(plane)] for z in range(depth)]
    along = [[z * plane + i for z in range(depth)] for i in range(plane)]

    def take(value):
        size = value.shape[-1] // plane
        return lax.dynamic_slice_in_dim(value, column * size, size, axis=value.ndim - 1)

    k_rows = w_x.shape[0]
    main = jnp.concatenate(
        [
            w_x.reshape(k_rows, plane, width),
            w_bc,
            w_dt.reshape(k_rows, plane, heads),
        ],
        axis=2,
    ).reshape(k_rows, -1)
    main = exchange_columns(main, in_plane, plane)
    main, tokens, w_z = lax.optimization_barrier((main, tokens, w_z))
    main = lax.all_gather(main, "ctx", axis=0, tiled=True, axis_index_groups=along)
    pieces = [tokens] + [swapped(tokens, step, plane) for step in range(1, plane)]
    w_gate = exchange_columns(w_z, in_plane, plane)
    w_gate = lax.all_gather(w_gate, "ctx", axis=0, tiled=True, axis_index_groups=along)
    rows = own_rows * plane
    blocks = rows // SPAN

    mixed = jnp.zeros((rows, width + bc_width), BF16)
    step_sum = jnp.zeros((rows, heads), F32)
    for step, piece in enumerate(pieces):
        projected = jnp.dot(piece, main, preferred_element_type=F32)
        at = ((column ^ step) * own_rows, 0)
        mixed = lax.dynamic_update_slice(
            mixed, projected[:, : width + bc_width].astype(BF16), at
        )
        step_sum = lax.dynamic_update_slice(step_sum, projected[:, width + bc_width :], at)
    edge = lax.ppermute(
        mixed[rows - (kernel - 1) :],
        "ctx",
        [(i, i + plane) for i in range(devices - plane)],
    )
    extended = jnp.concatenate([edge, mixed], axis=0)
    taps = jnp.concatenate([take(conv_x), take(conv_bc.reshape(kernel, -1))], axis=1)
    offset = jnp.concatenate([take(bias_x), take(bias_bc.reshape(-1))])
    running = jnp.zeros((rows, width + bc_width), F32) + offset[None, :]
    for tap in range(kernel):
        running = running + taps[tap][None, :] * extended[tap : tap + rows].astype(F32)
    conv = jax.nn.silu(running).astype(BF16)
    step = jax.nn.softplus(step_sum + take(dt_bias)[None, :])
    log_rate = -jnp.exp(take(a_log))[None, :] * step
    cumul = jnp.cumsum(log_rate.reshape(blocks, SPAN, heads), axis=1)
    step = step.reshape(blocks, SPAN, heads)
    block_log = cumul[:, -1, :]
    ending = (jnp.exp(block_log[:, None, :] - cumul) * step).reshape(rows, heads)
    before = jnp.cumsum(block_log, axis=0)
    reach = jnp.exp(cumul + (before - block_log)[:, None, :]).reshape(rows, heads)
    before = before[-1]
    scan, state = local_scan(
        conv,
        cumul.reshape(rows, heads),
        jnp.swapaxes(cumul, 1, 2),
        jnp.swapaxes(step, 1, 2),
        ending,
        jnp.repeat(jnp.exp(block_log), head_dim, axis=1)[:, None, :],
        jnp.repeat(take(d_skip), head_dim)[None, :],
        width,
        state_size,
        heads,
    )
    spread = jnp.repeat(jnp.eye(heads, dtype=F32), head_dim, axis=1)
    reach = jnp.dot(reach, spread, precision=lax.Precision.HIGHEST)

    high = lax.reduce_precision(before, 8, 7)
    low = before - high
    logs = jnp.stack([high, low]).astype(BF16)
    packed = jnp.concatenate(
        [
            state.astype(BF16),
            jnp.repeat(logs, head_dim, axis=1),
        ]
    )
    carried = jnp.zeros((state_size, width), F32)
    skipped = jnp.zeros((width,), F32)
    for part in earlier_parts(packed, along, plane, depth):
        part = part.astype(F32)
        carried = carried + jnp.exp(skipped)[None, :] * part[:state_size]
        skipped = skipped + part[state_size] + part[state_size + 1]
    far = jnp.dot(
        conv[:, width + state_size :], carried.astype(BF16), preferred_element_type=F32
    )
    scan = scan + far * reach

    scan, w_gate = lax.optimization_barrier((scan, w_gate))
    gain = take(norm_gain)[None, :]
    out = jnp.zeros((own_rows, plane * width), BF16)
    for step in reversed(range(plane)):
        gate = jnp.dot(pieces[step], w_gate, preferred_element_type=F32).astype(BF16)
        part = lax.dynamic_slice_in_dim(scan, (column ^ step) * own_rows, own_rows)
        gated = part * jax.nn.silu(gate.astype(F32))
        scale = lax.rsqrt(jnp.mean(gated * gated, axis=-1, keepdims=True) + 1e-05)
        result = (gated * scale * gain).astype(BF16)
        if step:
            result = swapped(result, step, plane)
        out = lax.dynamic_update_slice(out, result, (0, (column ^ step) * width))
    return out


def solution(mesh):
    placed = (
        P("ctx", None),
        P("ctx", "grp"),
        P("ctx", "grp"),
        P("ctx", "grp", None),
        P("ctx", "grp"),
        P(None, "grp"),
        P(None, "grp", None),
        P("grp"),
        P("grp", None),
        P("grp"),
        P("grp"),
        P("grp"),
        P("grp"),
    )
    return jax.shard_map(
        on_device, mesh=mesh, in_specs=placed, out_specs=P("ctx", "grp"), check_vma=False
    )
```

```python
import functools

import jax
import jax.numpy as jnp
from jax import lax
from jax.experimental import pallas as pl
from jax.experimental.pallas import tpu as pltpu
from jax.sharding import PartitionSpec as P

SPAN = 256
F32 = jnp.float32
BF16 = jnp.bfloat16


def exchange_columns(value, groups, count):
    if count == 1:
        return value
    rows = value.shape[0]
    parts = value.reshape(rows, count, -1)
    got = lax.all_to_all(
        parts.swapaxes(0, 1), "ctx", 0, 0, axis_index_groups=groups, tiled=True
    )
    return got.reshape(count * rows, -1)


def swapped(value, step, plane):
    pairs = [(i, i - i % plane + (i % plane ^ step)) for i in range(lax.axis_size("ctx"))]
    return lax.ppermute(value, "ctx", pairs)


def shared(value, step, plane):
    if lax.axis_size("grp") != 2:
        return swapped(value, step, plane)
    core = lax.axis_index("grp")
    half = value.shape[0] // 2
    got = swapped(lax.dynamic_slice_in_dim(value, core * half, half), step, plane)
    other = lax.ppermute(got, "grp", [(0, 1), (1, 0)])
    lower = jnp.where(core == 0, got, other)
    upper = jnp.where(core == 0, other, got)
    return jnp.concatenate([lower, upper])


def earlier_parts(value, along, plane, depth):
    if depth <= 4:
        for back in range(1, depth):
            pairs = [(i, i + back * plane) for i in range((depth - back) * plane)]
            yield lax.ppermute(value, "ctx", pairs)
    else:
        everyone = lax.all_gather(value, "ctx", axis_index_groups=along)
        level = lax.axis_index("ctx") // plane
        for back in range(1, depth):
            part = lax.dynamic_index_in_dim(
                everyone, jnp.maximum(level - back, 0), keepdims=False
            )
            yield jnp.where(back <= level, part, 0)


def scan_body(
    width, state_size, conv, cumul, cumul_t, step_t, ending, decay, skip, out, state
):
    @pl.when(pl.program_id(0) == 0)
    def _():
        state[...] = jnp.zeros_like(state)

    b_in = conv[:, width : width + state_size]
    c_in = conv[:, width + state_size :]
    scores = lax.dot_general(
        c_in, b_in, (((1,), (1,)), ((), ())), preferred_element_type=F32
    )
    row = lax.broadcasted_iota(jnp.int32, (SPAN, SPAN), 0)
    col = lax.broadcasted_iota(jnp.int32, (SPAN, SPAN), 1)
    scores = jnp.where(row >= col, scores, 0.0)
    first = lax.broadcasted_iota(jnp.int32, (SPAN, 128), 1) < 64
    for pair in range(width // 128):
        lanes = slice(pair * 128, pair * 128 + 128)
        x_in = conv[:, lanes]
        x_wide = x_in.astype(F32)
        sums = []
        for head in (2 * pair, 2 * pair + 1):
            gap = cumul[:, head : head + 1] - cumul_t[0, head : head + 1, :]
            weight = scores * jnp.exp(jnp.minimum(gap, 0.0)) * step_t[0, head : head + 1, :]
            sums.append(jnp.dot(weight.astype(BF16), x_in, preferred_element_type=F32))

        def both(ref):
            return jnp.where(
                first, ref[:, 2 * pair : 2 * pair + 1], ref[:, 2 * pair + 1 : 2 * pair + 2]
            )

        old = state[:, lanes]
        inter = jnp.dot(c_in, old.astype(BF16), preferred_element_type=F32)
        out[:, lanes] = (
            jnp.where(first, sums[0], sums[1])
            + inter * jnp.exp(both(cumul))
            + skip[:, lanes] * x_wide
        )
        scaled = (x_wide * both(ending)).astype(BF16)
        new = lax.dot_general(
            b_in, scaled, (((0,), (0,)), ((), ())), preferred_element_type=F32
        )
        state[:, lanes] = decay[0, :, lanes] * old + new


def local_scan(
    conv, cumul, cumul_t, step_t, ending, decay, skip, width, state_size, heads
):
    rows = conv.shape[0]
    return pl.pallas_call(
        functools.partial(scan_body, width, state_size),
        grid=(rows // SPAN,),
        in_specs=[
            pl.BlockSpec((SPAN, conv.shape[1]), lambda i: (i, 0)),
            pl.BlockSpec((SPAN, heads), lambda i: (i, 0)),
            pl.BlockSpec((1, heads, SPAN), lambda i: (i, 0, 0)),
            pl.BlockSpec((1, heads, SPAN), lambda i: (i, 0, 0)),
            pl.BlockSpec((SPAN, heads), lambda i: (i, 0)),
            pl.BlockSpec((1, 1, width), lambda i: (i, 0, 0)),
            pl.BlockSpec((1, width), lambda i: (0, 0)),
        ],
        out_specs=[
            pl.BlockSpec((SPAN, width), lambda i: (i, 0)),
            pl.BlockSpec((state_size, width), lambda i: (0, 0)),
        ],
        out_shape=[
            jax.ShapeDtypeStruct((rows, width), F32),
            jax.ShapeDtypeStruct((state_size, width), F32),
        ],
        compiler_params=pltpu.CompilerParams(vmem_limit_bytes=32 * 1024 * 1024),
        cost_estimate=pl.CostEstimate(
            flops=2 * rows * width * (SPAN + 2 * state_size),
            bytes_accessed=rows * width * 8,
            transcendentals=rows * SPAN * heads,
        ),
        name="local_scan",
    )(conv, cumul, cumul_t, step_t, ending, decay, skip)


def on_device(
    tokens,
    w_z,
    w_x,
    w_bc,
    w_dt,
    conv_x,
    conv_bc,
    bias_x,
    bias_bc,
    dt_bias,
    a_log,
    d_skip,
    norm_gain,
):
    own_rows = tokens.shape[0]
    kernel = conv_x.shape[0]
    group_count = w_bc.shape[1]
    bc_width = w_bc.shape[2]
    state_size = bc_width // 2
    heads = w_dt.shape[1] // group_count
    width = w_x.shape[1] // group_count
    head_dim = width // heads
    devices = lax.axis_size("ctx")
    plane = group_count
    depth = devices // plane
    mine = lax.axis_index("ctx")
    column = mine % plane
    in_plane = [[z * plane + i for i in range(plane)] for z in range(depth)]
    along = [[z * plane + i for z in range(depth)] for i in range(plane)]

    def take(value):
        size = value.shape[-1] // plane
        return lax.dynamic_slice_in_dim(value, column * size, size, axis=value.ndim - 1)

    k_rows = w_x.shape[0]
    main = jnp.concatenate(
        [
            w_x.reshape(k_rows, plane, width),
            w_bc,
            w_dt.reshape(k_rows, plane, heads),
        ],
        axis=2,
    ).reshape(k_rows, -1)
    main = exchange_columns(main, in_plane, plane)
    main, tokens, w_z = lax.optimization_barrier((main, tokens, w_z))
    main = lax.all_gather(main, "ctx", axis=0, tiled=True, axis_index_groups=along)
    pieces = [tokens] + [shared(tokens, step, plane) for step in range(1, plane)]
    w_gate = exchange_columns(w_z, in_plane, plane)
    w_gate = lax.all_gather(w_gate, "ctx", axis=0, tiled=True, axis_index_groups=along)
    rows = own_rows * plane
    blocks = rows // SPAN

    mixed = jnp.zeros((rows, width + bc_width), BF16)
    step_sum = jnp.zeros((rows, heads), F32)
    for step, piece in enumerate(pieces):
        projected = jnp.dot(piece, main, preferred_element_type=F32)
        at = ((column ^ step) * own_rows, 0)
        mixed = lax.dynamic_update_slice(
            mixed, projected[:, : width + bc_width].astype(BF16), at
        )
        step_sum = lax.dynamic_update_slice(step_sum, projected[:, width + bc_width :], at)
    edge = lax.ppermute(
        mixed[rows - (kernel - 1) :],
        "ctx",
        [(i, i + plane) for i in range(devices - plane)],
    )
    extended = jnp.concatenate([edge, mixed], axis=0)
    taps = jnp.concatenate([take(conv_x), take(conv_bc.reshape(kernel, -1))], axis=1)
    offset = jnp.concatenate([take(bias_x), take(bias_bc.reshape(-1))])
    running = jnp.zeros((rows, width + bc_width), F32) + offset[None, :]
    for tap in range(kernel):
        running = running + taps[tap][None, :] * extended[tap : tap + rows].astype(F32)
    conv = jax.nn.silu(running).astype(BF16)
    step = jax.nn.softplus(step_sum + take(dt_bias)[None, :])
    log_rate = -jnp.exp(take(a_log))[None, :] * step
    cumul = jnp.cumsum(log_rate.reshape(blocks, SPAN, heads), axis=1)
    step = step.reshape(blocks, SPAN, heads)
    block_log = cumul[:, -1, :]
    ending = (jnp.exp(block_log[:, None, :] - cumul) * step).reshape(rows, heads)
    before = jnp.cumsum(block_log, axis=0)
    reach = jnp.exp(cumul + (before - block_log)[:, None, :]).reshape(rows, heads)
    before = before[-1]
    scan, state = local_scan(
        conv,
        cumul.reshape(rows, heads),
        jnp.swapaxes(cumul, 1, 2),
        jnp.swapaxes(step, 1, 2),
        ending,
        jnp.repeat(jnp.exp(block_log), head_dim, axis=1)[:, None, :],
        jnp.repeat(take(d_skip), head_dim)[None, :],
        width,
        state_size,
        heads,
    )
    spread = jnp.repeat(jnp.eye(heads, dtype=F32), head_dim, axis=1)
    reach = jnp.dot(reach, spread, precision=lax.Precision.HIGHEST)

    high = lax.reduce_precision(before, 8, 7)
    low = before - high
    logs = jnp.stack([high, low]).astype(BF16)
    packed = jnp.concatenate(
        [
            state.astype(BF16),
            jnp.repeat(logs, head_dim, axis=1),
        ]
    )
    carried = jnp.zeros((state_size, width), F32)
    skipped = jnp.zeros((width,), F32)
    for part in earlier_parts(packed, along, plane, depth):
        part = part.astype(F32)
        carried = carried + jnp.exp(skipped)[None, :] * part[:state_size]
        skipped = skipped + part[state_size] + part[state_size + 1]
    far = jnp.dot(
        conv[:, width + state_size :], carried.astype(BF16), preferred_element_type=F32
    )
    scan = scan + far * reach

    scan, w_gate = lax.optimization_barrier((scan, w_gate))
    gain = take(norm_gain)[None, :]
    out = jnp.zeros((own_rows, plane * width), BF16)
    for step in reversed(range(plane)):
        gate = jnp.dot(pieces[step], w_gate, preferred_element_type=F32).astype(BF16)
        part = lax.dynamic_slice_in_dim(scan, (column ^ step) * own_rows, own_rows)
        gated = part * jax.nn.silu(gate.astype(F32))
        scale = lax.rsqrt(jnp.mean(gated * gated, axis=-1, keepdims=True) + 1e-05)
        result = (gated * scale * gain).astype(BF16)
        if step:
            result = swapped(result, step, plane)
        out = lax.dynamic_update_slice(out, result, (0, (column ^ step) * width))
    return out


def solution(mesh):
    placed = (
        P("ctx", None),
        P("ctx", "grp"),
        P("ctx", "grp"),
        P("ctx", "grp", None),
        P("ctx", "grp"),
        P(None, "grp"),
        P(None, "grp", None),
        P("grp"),
        P("grp", None),
        P("grp"),
        P("grp"),
        P("grp"),
        P("grp"),
    )
    return jax.shard_map(
        on_device, mesh=mesh, in_specs=placed, out_specs=P("ctx", "grp"), check_vma=False
    )
```
